512 devices in a mesh: replica: 32 (over z_lo, y), fsdp: 8 (over z_hi, x), tensor: 2 (over core).
Axes of the slice: x: 4, y: 4, z: 16 (z_hi: 2, z_lo: 8; z = z_hi * 8 + z_lo), core: 2. Of those that a mesh axis runs over, the one named last changes fastest.
Arguments:
- w_local: bfloat16 [32, 10240, 512], P('replica', 'fsdp', 'tensor'), may hold values from -24 to 24
- anchor: bfloat16 [10240, 512], P('fsdp', 'tensor'), may hold values from -20 to 20
- momentum: float32 [8, 32, 40, 512], P('fsdp', 'replica', None, 'tensor'), may hold values from -4 to 4
- key_grad: bfloat16 [32, 2304, 512], P('replica', 'fsdp', 'tensor'), may hold values from -0.25 to 0.25
Outputs:
- new_weights: bfloat16 [10240, 512], P('fsdp', 'tensor')
- new_momentum: float32 [8, 32, 40, 512], P('fsdp', 'replica', None, 'tensor')
- input_grad: bfloat16 [32, 8, 288, 10240], P('replica', None, 'tensor', 'fsdp')
- max_scale: float32 [1], replicated
The draws below stay inside these ranges and needn't reach their ends.
All inputs are finite; a program needn't handle non-finite values.
Results may differ from the reference program's by a relative error of at most 0.006.
Values may be sent and summed in bfloat16 or wider, within the bound.
No kernel may reach another device: no remote copies, remote signals or barrier semaphores. Data moves between devices by JAX's collectives and lax.ppermute only.
A program may use at most 64 MiB of HBM per device.

```python
import jax
import jax.numpy as jnp
from jax import lax

D = 10240
TOK_DEV = 288
KW = 512
TOKENS = 2304
ROWS = 40
N_REPLICA = 32
N_FSDP = 8


def shared_anchor(key):
    values = jax.random.normal(jax.random.fold_in(key, 101), (D, KW), jnp.float32)
    return jnp.clip(values, -20.0, 20.0)


def draw_anchor(key, part):
    return shared_anchor(key).astype(jnp.bfloat16)


def draw_w_local(key, part):
    anchor_values = shared_anchor(key)
    own_key = jax.random.fold_in(key, 7)
    common = 0.3 * jax.random.normal(jax.random.fold_in(own_key, 1), (1, D, KW), jnp.float32)
    single = 0.3 * jax.random.normal(jax.random.fold_in(own_key, 2), (N_REPLICA, D, KW), jnp.float32)
    replica_pos = jnp.arange(N_REPLICA)[:, None, None]
    rising = 1.0 + 2.0 * replica_pos.astype(jnp.float32) / max(N_REPLICA - 1, 1)
    row_pos = jnp.arange(D)[None, :, None]
    owner = row_pos % (D // N_FSDP) // ROWS
    spiked = jnp.where(owner == replica_pos, 3.0, 1.0).astype(jnp.float32)
    result = anchor_values[None] + common + single * rising * spiked
    return jnp.clip(result, -24.0, 24.0).astype(jnp.bfloat16)


def block_scale(stream_key, shape, shards, least, high):
    def one(dim, parts):
        draws = jax.random.uniform(jax.random.fold_in(jax.random.fold_in(stream_key, 6), dim), (parts,), jnp.float32, least / len(shards), high / len(shards))
        return jnp.repeat(jnp.exp(draws), shape[dim] // parts).reshape((-1,) + (1,) * (len(shape) - dim - 1))

    gain = one(*shards[0])
    for cut in shards[1:]:
        gain = gain * one(*cut)
    return gain


def noise(stream_key, extent, scale, reach, cuts=(), dtype=jnp.bfloat16):
    array = jax.random.normal(stream_key, extent, jnp.float32) * scale
    if len(cuts) > 0:
        array = block_scale(stream_key, extent, cuts, -0.22, 0.18) * array
    return jnp.clip(array, min=-reach, max=reach).astype(dtype)


def setup_inputs(seed: int = 0) -> dict:
    key_of = jax.random.split(jax.random.key(seed), 5)
    return {
        "w_local": draw_w_local(jax.random.fold_in(key_of[4], 71), 0),
        "anchor": draw_anchor(jax.random.fold_in(key_of[4], 71), 0),
        "momentum": noise(key_of[2], (N_FSDP, N_REPLICA, ROWS, KW), 0.3, 4.0, ((0, 8), (1, 32), (3, 2)), jnp.float32),
        "key_grad": noise(key_of[3], (N_REPLICA, TOKENS, KW), KW ** -0.5, 0.25, ((0, 32), (1, 8), (2, 2))),
    }


OUTER_MOMENTUM = 0.9
OUTER_RATE = 0.7
EPSILON = 1e-6


def reference(w_local, anchor, momentum, key_grad):
    anchor_wide = anchor.astype(jnp.float32)

    def replica_peak(weights):
        return jnp.max(jnp.abs(anchor_wide - weights.astype(jnp.float32)))

    max_scale = jnp.max(lax.map(replica_peak, w_local)) + EPSILON

    def accumulate(summed, weights):
        coded_grad = ((anchor_wide - weights.astype(jnp.float32)) / max_scale).astype(jnp.bfloat16)
        return summed + coded_grad.astype(jnp.float32), None

    summed, ignored = lax.scan(accumulate, jnp.zeros((D, KW), jnp.float32), w_local)
    mean_drift = summed * max_scale / N_REPLICA
    moment_new = OUTER_MOMENTUM * momentum.reshape(D, KW) + mean_drift
    new_weights = (anchor_wide - OUTER_RATE * (mean_drift + OUTER_MOMENTUM * moment_new)).astype(jnp.bfloat16)

    def project_replica(operands):
        gradients, weights = operands
        return jnp.dot(gradients, weights.T, preferred_element_type=jnp.float32).astype(jnp.bfloat16)

    input_grad = lax.map(project_replica, (key_grad, w_local))
    return (new_weights, moment_new.reshape(N_FSDP, N_REPLICA, ROWS, KW),
            input_grad.reshape(N_REPLICA, N_FSDP, TOK_DEV, D),
            jnp.reshape(max_scale, (1,)).astype(jnp.float32))
```

```python
import jax
import jax.numpy as jnp
from jax import lax
from jax.sharding import PartitionSpec as P

OUTER_MOMENTUM = 0.9
OUTER_RATE = 0.7
EPSILON = 1e-06
N_REPLICA = 32
STEP_GAIN = OUTER_RATE * (1.0 + OUTER_MOMENTUM) / N_REPLICA
MOMENTUM_GAIN = OUTER_MOMENTUM * OUTER_MOMENTUM * N_REPLICA / (1.0 + OUTER_MOMENTUM)
F32, BF16 = jnp.float32, jnp.bfloat16


def swap(x, axis, bit):
    n = lax.axis_size(axis)
    return lax.ppermute(x, axis, [(i, i ^ bit) for i in range(n)])


def pick(x, index, axis):
    return lax.dynamic_index_in_dim(x, index, axis, keepdims=False)


def body(w_local, anchor, momentum, key_grad):
    r = lax.axis_index("replica")
    y, hi, lo = r & 3, r >> 4, (r >> 2) & 3
    f = lax.axis_index("fsdp")
    t = lax.axis_index("tensor")
    w = w_local[0]
    cols = w.shape[1]

    kg = key_grad[0]
    tokens = kg.shape[0]
    half = tokens // 2
    pair = jnp.stack([kg, swap(kg, "fsdp", 4)])
    rows = jnp.concatenate([pair] + [swap(pair, "fsdp", d) for d in (1, 2, 3)])
    rows = rows.reshape(8, 2, half, cols)
    mine, theirs = pick(rows, t, 1), pick(rows, 1 - t, 1)
    other = swap(theirs, "tensor", 1)
    w_other = swap(w, "tensor", 1)
    dims = (((2,), (1,)), ((), ()))

    w4 = w.reshape(8, 4, 40, cols)
    a4 = anchor.reshape(8, 4, 40, cols)
    a_y = pick(a4, y, 1).astype(F32)
    parts = [pick(w4, y, 1)] + [swap(pick(w4, y ^ d, 1), "replica", d) for d in (1, 2, 3)]
    p1 = sum(a_y - p.astype(F32) for p in parts)
    p1 = p1.reshape(2, 4, 40, cols)
    send = pick(p1, 1 - hi, 0).astype(BF16)
    p2 = pick(p1, hi, 0) + swap(send, "replica", 16).astype(F32)
    m = momentum[0, 0]
    own = lax.broadcasted_iota(jnp.int32, (4, 1, 1), 0) == lo
    q = (p2 + jnp.where(own, MOMENTUM_GAIN * m[None], 0.0)).astype(BF16)
    got = [swap(q, "replica", 4 * d).astype(F32) for d in (1, 2, 3)]
    total = (q.astype(F32) + got[0]) + (got[1] + got[2])
    summed = pick(p2, lo, 0) + sum(pick(g, lo, 0) for g in got)
    moment_new = OUTER_MOMENTUM * m + summed / N_REPLICA
    a_hi = pick(a_y.reshape(2, 4, 40, cols), hi, 0)
    fresh = (a_hi - STEP_GAIN * total).astype(BF16)
    far = swap(fresh, "replica", 16)
    eight = jnp.where(hi == 0, jnp.stack([fresh, far]), jnp.stack([far, fresh])).reshape(8, 40, cols)
    pieces = [eight] + [swap(eight, "replica", d) for d in (1, 2, 3)]
    out = jnp.zeros((8, 4, 40, cols), BF16)
    for d in range(4):
        out = lax.dynamic_update_index_in_dim(out, pieces[d], y ^ d, 1)
    new_weights = out.reshape(1280, cols)

    scale = jnp.max(jnp.abs(anchor.astype(F32) - w.astype(F32)))
    scale = jnp.full((8, 128), scale, F32)
    for axis, masks in (("tensor", (1,)), ("replica", (1, 2, 3)), ("replica", (4, 8, 12)), ("replica", (16,)), ("fsdp", (4,)), ("fsdp", (1, 2, 3))):
        got_s = [swap(scale, axis, k) for k in masks]
        for g in got_s:
            scale = jnp.maximum(scale, g)
    max_scale = scale[0, :1] + EPSILON

    where = jnp.array([0, 2, 4, 6, 1, 3, 5, 7])[jnp.arange(8) ^ f]
    a_in = jnp.take(jnp.concatenate([mine, other], axis=2), where, axis=0)
    w_in = jnp.concatenate([w, w_other], axis=1)
    prod = lax.dot_general(a_in, w_in, dims, preferred_element_type=F32).astype(BF16)
    input_grad = prod[None]
    return new_weights, moment_new[None, None], input_grad, max_scale


def solution(mesh):
    return jax.shard_map(
        body,
        mesh=mesh,
        in_specs=(
            P("replica", "fsdp", "tensor"),
            P("fsdp", "tensor"),
            P("fsdp", "replica", None, "tensor"),
            P("replica", "fsdp", "tensor"),
        ),
        out_specs=(
            P("fsdp", "tensor"),
            P("fsdp", "replica", None, "tensor"),
            P("replica", None, "tensor", "fsdp"),
            P(),
        ),
        check_vma=False,
    )
```

```python
import jax
import jax.numpy as jnp
from jax import lax
from jax.experimental import pallas as pl
from jax.experimental.pallas import tpu as pltpu
from jax.sharding import PartitionSpec as P

OUTER_MOMENTUM = 0.9
OUTER_RATE = 0.7
EPSILON = 1e-06
N_REPLICA = 32
STEP_GAIN = OUTER_RATE * (1.0 + OUTER_MOMENTUM) / N_REPLICA
MOMENTUM_GAIN = OUTER_MOMENTUM * OUTER_MOMENTUM * N_REPLICA / (1.0 + OUTER_MOMENTUM)
F32, BF16 = jnp.float32, jnp.bfloat16
ROWS, COLS, TAIL, TOK = 40, 256, 16, 144
TOP = (8, COLS)
VMEM = pl.BlockSpec(memory_space=pltpu.VMEM)
SMEM = pl.BlockSpec(memory_space=pltpu.SMEM)


def swap(x, axis, bit):
    n = lax.axis_size(axis)
    return lax.ppermute(x, axis, [(i, i ^ bit) for i in range(n)])


def tie(x, dep):
    return lax.optimization_barrier((x, dep))[0]


def call(kernel, outs, args, scratch=()):
    return pl.pallas_call(
        kernel,
        out_shape=[jax.ShapeDtypeStruct(s, d) for s, d in outs],
        in_specs=[SMEM] + [VMEM] * (len(args) - 1),
        out_specs=[VMEM] * len(outs),
        scratch_shapes=[pltpu.VMEM(s, d) for s, d in scratch],
        compiler_params=pltpu.CompilerParams(vmem_limit_bytes=24 * 1024 * 1024),
    )(*args)


def tail(m):
    a = m.astype(BF16).astype(F32)
    b = (m - a).astype(BF16).astype(F32)
    c = m - a - b
    row = lax.broadcasted_iota(jnp.int32, (TAIL, COLS), 0)
    return jnp.where(row == 0, a, jnp.where(row == 1, b, c)).astype(BF16)


def untail(ref, rows):
    p = ref[rows : rows + TAIL].astype(F32)
    return p[0:1] + p[1:2] + p[2:3]


def put(msg, rows, m):
    n = rows.shape[0]
    msg[0:n] = rows.astype(BF16)
    msg[n : n + TAIL] = tail(m)


def start_kernel(ix, w, a, kg, m1, m2, m3, own, a_y, kgm, mx):
    y = ix[0]
    top = jnp.zeros(TOP, F32)
    for i in range(8):
        d = jnp.abs(a[i].astype(F32) - w[i].astype(F32)).reshape(-1, 8, COLS)
        top = jnp.maximum(top, jnp.max(d, axis=0))
    m = jnp.broadcast_to(jnp.max(top), (1, COLS))
    kgm[0 : 2 * TOK] = kg[...]
    kgm[2 * TOK :] = tail(m)
    for d, msg in ((1, m1), (2, m2), (3, m3)):
        msg[...] = w[:, y ^ d].astype(F32).reshape(8 * ROWS, COLS).astype(BF16)
    mine = a[:, y].astype(F32).reshape(8 * ROWS, COLS)
    a_y[...] = mine
    own[...] = mine - w[:, y].astype(F32).reshape(8 * ROWS, COLS)
    mx[...] = jnp.broadcast_to(m, TOP)


def y_kernel(ix, own, a_y, g1, g2, g3, h, own4, s):
    lo = ix[2]
    mine = a_y[...]
    s[...] = own[...] + sum(mine - g[...].astype(F32) for g in (g1, g2, g3))

    def blocks(k):
        return [s[pl.ds((4 * b + k) * ROWS, ROWS)] for b in range(2)]

    h[...] = jnp.concatenate(blocks(lo ^ 1) + blocks(lo ^ 3)).astype(BF16)
    own4[...] = jnp.concatenate(blocks(lo) + blocks(lo ^ 2))


def near_kernel(ix, own4, g, h, own2):
    s = own4[...] + g[...].astype(F32)
    h[...] = s[2 * ROWS :].astype(BF16)
    own2[...] = s[: 2 * ROWS]


def lo_kernel(ix, own2, mom, h, mx, mr, q, p_own, mx2, s):
    hi = ix[1]
    m = jnp.maximum(mx[0:1], mr[0:1])
    s[...] = own2[...] + h[...].astype(F32)
    here = pl.ds(hi * ROWS, ROWS)
    p_own[...] = s[here]
    s[here] = s[here] + MOMENTUM_GAIN * mom[...]
    put(q, s[...], m)
    mx2[...] = jnp.broadcast_to(m, TOP)


def hi_kernel(ix, q, p_own, mom, a_y, mx, g, fresh, mom_new, mx2, s):
    hi, lo = ix[1], ix[2]
    m = jnp.maximum(mx[0:1], untail(g, 2 * ROWS))
    s[...] = g[0 : 2 * ROWS].astype(F32)
    total = q[0 : 2 * ROWS].astype(F32) + s[...]
    summed = p_own[...] + s[pl.ds(hi * ROWS, ROWS)]
    mom_new[...] = OUTER_MOMENTUM * mom[...] + summed * (1.0 / N_REPLICA)
    rows = jnp.concatenate([a_y[pl.ds((4 * b + lo) * ROWS, ROWS)] for b in range(2)])
    put(fresh, rows - STEP_GAIN * total, m)
    mx2[...] = jnp.broadcast_to(m, TOP)


def join_kernel(ix, a, b, mx, out, mx2):
    n = b.shape[0] - TAIL
    m = jnp.maximum(mx[0:1], untail(b, n))
    out[0:n] = a[0:n]
    out[n : 2 * n] = b[0:n]
    out[2 * n :] = tail(m)
    mx2[...] = jnp.broadcast_to(m, TOP)


def eight_kernel(ix, near, far, mx, eight, mx2, s):
    lo = ix[2]
    for j, ref in enumerate((near, far)):
        x = ref[0 : 4 * ROWS].astype(F32)
        for k in range(2):
            for b in range(2):
                at = (2 * k + b) * ROWS
                s[pl.ds((4 * b + (lo ^ (j + 2 * k))) * ROWS, ROWS)] = x[at : at + ROWS]
    m = jnp.maximum(mx[0:1], untail(far, 4 * ROWS))
    put(eight, s[...], m)
    mx2[...] = jnp.broadcast_to(m, TOP)


def out_kernel(ix, two, more, mx, out, scale):
    y = ix[0]
    n = 8 * ROWS
    for d, (ref, k) in enumerate(((two, 0), (two, 1), (more, 1), (more, 0))):
        out[:, y ^ d] = ref[k * n : (k + 1) * n].astype(F32).reshape(8, ROWS, COLS).astype(BF16)
    m = jnp.maximum(mx[0:1], untail(more, 2 * n))
    scale[...] = jnp.broadcast_to(m, TOP) + EPSILON


def pair_kernel(ix, a, b, mx, theirs, mine, mx2):
    t = ix[4]
    m = jnp.maximum(mx[0:1], untail(b, 2 * TOK))
    for i, ref in enumerate((a, b)):
        at = slice(i * TOK, (i + 1) * TOK)
        theirs[at] = ref[pl.ds(pl.multiple_of((1 - t) * TOK, 16), TOK)]
        mine[at] = ref[pl.ds(pl.multiple_of(t * TOK, 16), TOK)]
    theirs[2 * TOK :] = tail(m)
    mx2[...] = jnp.broadcast_to(m, TOP)


def core_kernel(ix, mine, g, mx, both, mx2):
    both[0 : 2 * TOK] = mine[...]
    both[2 * TOK :] = g[0 : 2 * TOK]
    mx2[...] = jnp.broadcast_to(jnp.maximum(mx[0:1], untail(g, 2 * TOK))[:, :128], (8, 128))


def quad_kernel(ix, a, b, quad):
    n = 2 * TOK
    for k in range(2):
        quad[2 * k * n : (2 * k + 1) * n] = a[k * n : (k + 1) * n]
        quad[(2 * k + 1) * n : (2 * k + 2) * n] = b[k * n : (k + 1) * n]


def product_kernel(place, a, b, wa, wb, out):
    dims = (((1,), (1,)), ((), ()))
    n = 4 * TOK
    for j, ref in enumerate((a, b)):
        x = lax.dot_general(ref[0:n], wa[...], dims, preferred_element_type=F32)
        x += lax.dot_general(ref[n:], wb[...], dims, preferred_element_type=F32)
        x = x.astype(BF16)
        for i in range(4):
            out[place[4 * j + i]] = x[i * TOK : (i + 1) * TOK]


def product(place, quad, more, w, w_other):
    width = w.shape[0]
    whole = pl.BlockSpec((8 * TOK, COLS), lambda i, s: (0, 0))
    part = pl.BlockSpec((COLS, COLS), lambda i, s: (i, 0))
    return pl.pallas_call(
        product_kernel,
        grid_spec=pltpu.PrefetchScalarGridSpec(
            num_scalar_prefetch=1,
            grid=(width // COLS,),
            in_specs=[whole, whole, part, part],
            out_specs=pl.BlockSpec((8, TOK, COLS), lambda i, s: (0, 0, i)),
        ),
        out_shape=jax.ShapeDtypeStruct((8, TOK, width), BF16),
        compiler_params=pltpu.CompilerParams(vmem_limit_bytes=24 * 1024 * 1024),
        cost_estimate=pl.CostEstimate(flops=16 * TOK * width * 2 * COLS, bytes_accessed=5_600_000, transcendentals=0),
    )(place, quad, more, w, w_other)


def body(w_local, anchor, momentum, key_grad):
    r = lax.axis_index("replica")
    f = lax.axis_index("fsdp")
    t = lax.axis_index("tensor")
    ix = jnp.stack([r & 3, r >> 4, (r >> 2) & 3, f, t])
    w = w_local[0]
    mom = momentum[0, 0]
    top = (TOP, F32)

    def bf(n):
        return ((n, COLS), BF16)

    def fl(n):
        return ((n, COLS), F32)

    w_other = swap(w, "tensor", 1)
    four = (8, 4, ROWS, COLS)
    m1, m2, m3, own, a_y, kgm, mx = call(
        start_kernel,
        [bf(320)] * 3 + [fl(320)] * 2 + [bf(304), top],
        (ix, w.reshape(four), anchor.reshape(four), key_grad[0]),
    )
    kg_far = swap(kgm, "fsdp", 4)
    g2, g1, g3 = (swap(m, "replica", d) for d, m in ((2, m2), (1, m1), (3, m3)))
    h, own4 = call(y_kernel, [bf(160), fl(160)], (ix, own, a_y, g1, g2, g3), [fl(320)])
    h = swap(h, "replica", 4)
    theirs, kg_mine, mx = call(pair_kernel, [bf(304), bf(288), top], (ix, kgm, kg_far, mx))
    kg_core = swap(theirs, "tensor", 1)
    h, own2 = call(near_kernel, [bf(80), fl(80)], (ix, own4, h))
    h = swap(h, "replica", 8)
    both, ms = call(core_kernel, [bf(576), ((8, 128), F32)], (ix, kg_mine, kg_core, mx))
    ms = jnp.maximum(ms, swap(ms, "fsdp", 1))
    mr = swap(ms, "fsdp", 3)
    wide = [jnp.concatenate([m, m], axis=1) for m in (ms, mr)]
    q, p_own, mx = call(lo_kernel, [bf(96), fl(40), top], (ix, own2, mom, h, *wide), [fl(80)])
    g = swap(q, "replica", 16)
    kg_x = swap(tie(both, q), "fsdp", 1)
    fresh, mom_new, mx = call(hi_kernel, [bf(96), fl(40), top], (ix, q, p_own, mom, a_y, mx, g), [fl(80)])
    near, mx = call(join_kernel, [bf(176), top], (ix, fresh, swap(fresh, "replica", 8), mx))
    far = swap(near, "replica", 4)
    quad = call(quad_kernel, [bf(1152)], (ix, both, tie(kg_x, near)))[0]
    more = swap(quad, "fsdp", 3)
    eight, mx = call(eight_kernel, [bf(336), top], (ix, near, far, mx), [fl(320)])
    two, mx = call(join_kernel, [bf(656), top], (ix, eight, swap(eight, "replica", 1), mx))
    last = swap(two, "replica", 3)
    place = jnp.array([0, 4, 1, 5, 3, 7, 2, 6], jnp.int32) ^ f
    prod = product(place, quad, tie(more, two), w, w_other)
    new_weights, scale = call(out_kernel, [(four, BF16), top], (ix, two, tie(last, prod), mx))
    return new_weights.reshape(anchor.shape), mom_new[None, None], prod[None], scale[0, :1]


def solution(mesh):
    return jax.shard_map(
        body,
        mesh=mesh,
        in_specs=(
            P("replica", "fsdp", "tensor"),
            P("fsdp", "tensor"),
            P("fsdp", "replica", None, "tensor"),
            P("replica", "fsdp", "tensor"),
        ),
        out_specs=(
            P("fsdp", "tensor"),
            P("fsdp", "replica", None, "tensor"),
            P("replica", None, "tensor", "fsdp"),
            P(),
        ),
        check_vma=False,
    )
```

```python
import jax
import jax.numpy as jnp
from jax import lax
from jax.experimental import pallas as pl
from jax.experimental.pallas import tpu as pltpu
from jax.sharding import PartitionSpec as P

OUTER_MOMENTUM = 0.9
OUTER_RATE = 0.7
EPSILON = 1e-06
N_REPLICA = 32
STEP_GAIN = OUTER_RATE * (1.0 + OUTER_MOMENTUM) / N_REPLICA
MOMENTUM_GAIN = OUTER_MOMENTUM * OUTER_MOMENTUM * N_REPLICA / (1.0 + OUTER_MOMENTUM)
F32, BF16 = jnp.float32, jnp.bfloat16
ROWS, COLS, TAIL, TOK = 40, 256, 16, 144
TOP = (8, COLS)
VMEM = pl.BlockSpec(memory_space=pltpu.VMEM)
SMEM = pl.BlockSpec(memory_space=pltpu.SMEM)


def swap(x, axis, bit):
    n = lax.axis_size(axis)
    return lax.ppermute(x, axis, [(i, i ^ bit) for i in range(n)])


def tie(x, dep):
    return lax.optimization_barrier((x, dep))[0]


def call(kernel, outs, args, scratch=(), micros=0.5):
    return pl.pallas_call(
        kernel,
        out_shape=[jax.ShapeDtypeStruct(s, d) for s, d in outs],
        in_specs=[SMEM] + [VMEM] * (len(args) - 1),
        out_specs=[VMEM] * len(outs),
        scratch_shapes=[pltpu.VMEM(s, d) for s, d in scratch],
        compiler_params=pltpu.CompilerParams(vmem_limit_bytes=24 * 1024 * 1024),
        cost_estimate=pl.CostEstimate(flops=int(micros * 1e9), bytes_accessed=0, transcendentals=0),
    )(*args)


def tail(m):
    a = m.astype(BF16).astype(F32)
    b = (m - a).astype(BF16).astype(F32)
    c = m - a - b
    row = lax.broadcasted_iota(jnp.int32, (TAIL, COLS), 0)
    return jnp.where(row == 0, a, jnp.where(row == 1, b, c)).astype(BF16)


def untail(ref, rows):
    p = ref[rows : rows + TAIL].astype(F32)
    return p[0:1] + p[1:2] + p[2:3]


def put(msg, rows, m):
    n = rows.shape[0]
    msg[0:n] = rows.astype(BF16)
    msg[n : n + TAIL] = tail(m)


def start_kernel(ix, w, a, kg, m1, m2, m3, own, a_y, kgm, mx):
    y = ix[0]
    top = jnp.zeros(TOP, F32)
    for i in range(8):
        d = jnp.abs(a[i].astype(F32) - w[i].astype(F32)).reshape(-1, 8, COLS)
        top = jnp.maximum(top, jnp.max(d, axis=0))
    m = jnp.broadcast_to(jnp.max(top), (1, COLS))
    kgm[0 : 2 * TOK] = kg[...]
    kgm[2 * TOK :] = tail(m)
    for d, msg in ((1, m1), (2, m2), (3, m3)):
        msg[...] = w[:, y ^ d].astype(F32).reshape(8 * ROWS, COLS).astype(BF16)
    mine = a[:, y].astype(F32).reshape(8 * ROWS, COLS)
    a_y[...] = mine
    own[...] = mine - w[:, y].astype(F32).reshape(8 * ROWS, COLS)
    mx[...] = jnp.broadcast_to(m, TOP)


def y_kernel(ix, own, a_y, g1, g2, g3, h, own4, s):
    lo = ix[2]
    mine = a_y[...]
    s[...] = own[...] + sum(mine - g[...].astype(F32) for g in (g1, g2, g3))

    def blocks(k):
        return [s[pl.ds((4 * b + k) * ROWS, ROWS)] for b in range(2)]

    h[...] = jnp.concatenate(blocks(lo ^ 1) + blocks(lo ^ 3)).astype(BF16)
    own4[...] = jnp.concatenate(blocks(lo) + blocks(lo ^ 2))


def near_kernel(ix, own4, g, h, own2):
    s = own4[...] + g[...].astype(F32)
    h[...] = s[2 * ROWS :].astype(BF16)
    own2[...] = s[: 2 * ROWS]


def lo_kernel(ix, own2, mom, h, mx, mr, q, p_own, mx2, s):
    hi = ix[1]
    m = jnp.maximum(mx[0:1], mr[0:1])
    s[...] = own2[...] + h[...].astype(F32)
    here = pl.ds(hi * ROWS, ROWS)
    p_own[...] = s[here]
    s[here] = s[here] + MOMENTUM_GAIN * mom[...]
    put(q, s[...], m)
    mx2[...] = jnp.broadcast_to(m, TOP)


def hi_kernel(ix, q, p_own, mom, a_y, mx, g, fresh, mom_new, mx2, s):
    hi, lo = ix[1], ix[2]
    m = jnp.maximum(mx[0:1], untail(g, 2 * ROWS))
    s[...] = g[0 : 2 * ROWS].astype(F32)
    total = q[0 : 2 * ROWS].astype(F32) + s[...]
    summed = p_own[...] + s[pl.ds(hi * ROWS, ROWS)]
    mom_new[...] = OUTER_MOMENTUM * mom[...] + summed * (1.0 / N_REPLICA)
    rows = jnp.concatenate([a_y[pl.ds((4 * b + lo) * ROWS, ROWS)] for b in range(2)])
    put(fresh, rows - STEP_GAIN * total, m)
    mx2[...] = jnp.broadcast_to(m, TOP)


def join_kernel(ix, a, b, mx, out, mx2):
    n = b.shape[0] - TAIL
    m = jnp.maximum(mx[0:1], untail(b, n))
    out[0:n] = a[0:n]
    out[n : 2 * n] = b[0:n]
    out[2 * n :] = tail(m)
    mx2[...] = jnp.broadcast_to(m, TOP)


def eight_kernel(ix, near, far, mx, eight, mx2, s):
    lo = ix[2]
    for j, ref in enumerate((near, far)):
        x = ref[0 : 4 * ROWS].astype(F32)
        for k in range(2):
            for b in range(2):
                at = (2 * k + b) * ROWS
                s[pl.ds((4 * b + (lo ^ (j + 2 * k))) * ROWS, ROWS)] = x[at : at + ROWS]
    m = jnp.maximum(mx[0:1], untail(far, 4 * ROWS))
    put(eight, s[...], m)
    mx2[...] = jnp.broadcast_to(m, TOP)


def out_kernel(ix, e0, e1, e2, e3, mx, out, scale):
    y = ix[0]
    n = 8 * ROWS
    m = mx[0:1]
    for d, e in enumerate((e0, e1, e2, e3)):
        out[:, y ^ d] = e[0:n].astype(F32).reshape(8, ROWS, COLS).astype(BF16)
        if d > 0:
            m = jnp.maximum(m, untail(e, n))
    scale[...] = jnp.broadcast_to(m, TOP) + EPSILON


def pair_kernel(ix, a, b, mx, theirs, mine, mx2):
    t = ix[4]
    m = jnp.maximum(mx[0:1], untail(b, 2 * TOK))
    for i, ref in enumerate((a, b)):
        at = slice(i * TOK, (i + 1) * TOK)
        theirs[at] = ref[pl.ds(pl.multiple_of((1 - t) * TOK, 16), TOK)]
        mine[at] = ref[pl.ds(pl.multiple_of(t * TOK, 16), TOK)]
    theirs[2 * TOK :] = tail(m)
    mx2[...] = jnp.broadcast_to(m, TOP)


def core_kernel(ix, mine, g, mx, both, mx2):
    both[0 : 2 * TOK] = mine[...]
    both[2 * TOK :] = g[0 : 2 * TOK]
    mx2[...] = jnp.broadcast_to(jnp.maximum(mx[0:1], untail(g, 2 * TOK))[:, :128], (8, 128))


def quad_kernel(ix, a, b, quad):
    n = 2 * TOK
    for k in range(2):
        quad[2 * k * n : (2 * k + 1) * n] = a[k * n : (k + 1) * n]
        quad[(2 * k + 1) * n : (2 * k + 2) * n] = b[k * n : (k + 1) * n]


def product_kernel(place, a, wa, wb, *rest):
    out, buf, sem = rest[-3:]
    dims = (((1,), (1,)), ((), ()))
    n = 4 * TOK
    copies = []
    for j in range(wa.shape[0] // COLS):
        at = slice(j * COLS, (j + 1) * COLS)
        x = lax.dot_general(a[0:n], wa[at], dims, preferred_element_type=F32)
        x += lax.dot_general(a[n:], wb[at], dims, preferred_element_type=F32)
        buf[j] = x.astype(BF16)
        for i in range(4):
            src = buf.at[j, pl.ds(i * TOK, TOK)]
            copy = pltpu.make_async_copy(src, out.at[place[i], :, pl.ds(j * COLS, COLS)], sem.at[j, i])
            copy.start()
            copies.append(copy)
    for copy in copies:
        copy.wait()


def product(place, rows, w, w_other, prod=None):
    width = w.shape[0]
    blocks = width // COLS
    args = [place, rows, w, w_other] + ([] if prod is None else [prod])
    return pl.pallas_call(
        product_kernel,
        in_specs=[SMEM, VMEM, VMEM, VMEM] + [pl.BlockSpec(memory_space=pl.ANY)] * (len(args) - 4),
        out_specs=pl.BlockSpec(memory_space=pl.ANY),
        out_shape=jax.ShapeDtypeStruct((8, TOK, width), BF16),
        scratch_shapes=[
            pltpu.VMEM((blocks, 4 * TOK, COLS), BF16),
            pltpu.SemaphoreType.DMA((blocks, 4)),
        ],
        input_output_aliases={} if prod is None else {4: 0},
        compiler_params=pltpu.CompilerParams(vmem_limit_bytes=24 * 1024 * 1024),
        cost_estimate=pl.CostEstimate(flops=8 * TOK * width * 2 * COLS, bytes_accessed=3_500_000, transcendentals=0),
    )(*args)


def body(w_local, anchor, momentum, key_grad):
    r = lax.axis_index("replica")
    f = lax.axis_index("fsdp")
    t = lax.axis_index("tensor")
    ix = jnp.stack([r & 3, r >> 4, (r >> 2) & 3, f, t])
    w = w_local[0]
    mom = momentum[0, 0]
    top = (TOP, F32)

    def bf(n):
        return ((n, COLS), BF16)

    def fl(n):
        return ((n, COLS), F32)

    w_other = swap(w, "tensor", 1)
    four = (8, 4, ROWS, COLS)
    m1, m2, m3, own, a_y, kgm, mx = call(
        start_kernel,
        [bf(320)] * 3 + [fl(320)] * 2 + [bf(304), top],
        (ix, w.reshape(four), anchor.reshape(four), key_grad[0]),
    )
    kg_far = swap(kgm, "fsdp", 4)
    g2, g1, g3 = (swap(m, "replica", d) for d, m in ((2, m2), (1, m1), (3, m3)))
    h, own4 = call(y_kernel, [bf(160), fl(160)], (ix, own, a_y, g1, g2, g3), [fl(320)])
    theirs, kg_mine, mx = call(pair_kernel, [bf(304), bf(288), top], (ix, kgm, kg_far, mx))
    h = swap(h, "replica", 4)
    kg_core = swap(theirs, "tensor", 1)
    h, own2 = call(near_kernel, [bf(80), fl(80)], (ix, own4, h))
    h = swap(h, "replica", 8)
    both, ms = call(core_kernel, [bf(576), ((8, 128), F32)], (ix, kg_mine, kg_core, mx))
    ms = jnp.maximum(ms, swap(ms, "fsdp", 1))
    mr = swap(ms, "fsdp", 3)
    wide = [jnp.concatenate([m, m], axis=1) for m in (ms, mr)]
    q, p_own, mx = call(lo_kernel, [bf(96), fl(40), top], (ix, own2, mom, h, *wide), [fl(80)])
    g = swap(q, "replica", 16)
    kg_x = swap(tie(both, q), "fsdp", 1)
    fresh, mom_new, mx = call(hi_kernel, [bf(96), fl(40), top], (ix, q, p_own, mom, a_y, mx, g), [fl(80)], 6.0)
    near, mx = call(join_kernel, [bf(176), top], (ix, fresh, swap(fresh, "replica", 8), mx))
    far = swap(near, "replica", 4)
    quad = call(quad_kernel, [bf(1152)], (ix, both, tie(kg_x, fresh)))[0]
    more = swap(quad, "fsdp", 3)
    place = jnp.array([0, 4, 1, 5, 3, 7, 2, 6], jnp.int32) ^ f
    prod = product(place[:4], quad, w, w_other)
    eight, mx = call(eight_kernel, [bf(336), top], (ix, near, tie(far, prod), mx), [fl(320)])
    e2, e1, e3 = (swap(eight, "replica", d) for d in (2, 1, 3))
    prod = product(place[4:], tie(more, eight), w, w_other, prod)
    new_weights, scale = call(out_kernel, [(four, BF16), top], (ix, eight, e1, tie(e2, prod), e3, mx))
    return new_weights.reshape(anchor.shape), mom_new[None, None], prod[None], scale[0, :1]


def solution(mesh):
    return jax.shard_map(
        body,
        mesh=mesh,
        in_specs=(
            P("replica", "fsdp", "tensor"),
            P("fsdp", "tensor"),
            P("fsdp", "replica", None, "tensor"),
            P("replica", "fsdp", "tensor"),
        ),
        out_specs=(
            P("fsdp", "tensor"),
            P("fsdp", "replica", None, "tensor"),
            P("replica", None, "tensor", "fsdp"),
            P(),
        ),
        check_vma=False,
    )
```

```python
import jax
import jax.numpy as jnp
from jax import lax
from jax.experimental import pallas as pl
from jax.experimental.pallas import tpu as pltpu
from jax.sharding import PartitionSpec as P

OUTER_MOMENTUM = 0.9
OUTER_RATE = 0.7
EPSILON = 1e-06
N_REPLICA = 32
STEP_GAIN = OUTER_RATE * (1.0 + OUTER_MOMENTUM) / N_REPLICA
MOMENTUM_GAIN = OUTER_MOMENTUM * OUTER_MOMENTUM * N_REPLICA / (1.0 + OUTER_MOMENTUM)
F32, BF16 = jnp.float32, jnp.bfloat16
ROWS, COLS, TAIL, TOK = 40, 256, 16, 144
TOP = (8, COLS)
VMEM = pl.BlockSpec(memory_space=pltpu.VMEM)
SMEM = pl.BlockSpec(memory_space=pltpu.SMEM)


def swap(x, axis, bit):
    n = lax.axis_size(axis)
    return lax.ppermute(x, axis, [(i, i ^ bit) for i in range(n)])


def tie(x, dep):
    return lax.optimization_barrier((x, dep))[0]


def call(kernel, outs, args, scratch=(), micros=0.5):
    return pl.pallas_call(
        kernel,
        out_shape=[jax.ShapeDtypeStruct(s, d) for s, d in outs],
        in_specs=[SMEM] + [VMEM] * (len(args) - 1),
        out_specs=[VMEM] * len(outs),
        scratch_shapes=[pltpu.VMEM(s, d) for s, d in scratch],
        compiler_params=pltpu.CompilerParams(vmem_limit_bytes=24 * 1024 * 1024),
        cost_estimate=pl.CostEstimate(flops=int(micros * 1e9), bytes_accessed=0, transcendentals=0),
    )(*args)


def tail(m):
    a = m.astype(BF16).astype(F32)
    b = (m - a).astype(BF16).astype(F32)
    c = m - a - b
    row = lax.broadcasted_iota(jnp.int32, (TAIL, COLS), 0)
    return jnp.where(row == 0, a, jnp.where(row == 1, b, c)).astype(BF16)


def untail(ref, rows):
    p = ref[rows : rows + TAIL].astype(F32)
    return p[0:1] + p[1:2] + p[2:3]


def put(msg, rows, m):
    n = rows.shape[0]
    msg[0:n] = rows.astype(BF16)
    msg[n : n + TAIL] = tail(m)


def start_kernel(ix, w, a, kg, m1, m2, m3, own, a_y, kgm, mx):
    y = ix[0]
    top = jnp.zeros(TOP, F32)
    for i in range(8):
        d = jnp.abs(a[i].astype(F32) - w[i].astype(F32)).reshape(-1, 8, COLS)
        top = jnp.maximum(top, jnp.max(d, axis=0))
    m = jnp.broadcast_to(jnp.max(top), (1, COLS))
    kgm[0 : 2 * TOK] = kg[...]
    kgm[2 * TOK :] = tail(m)
    for d, msg in ((1, m1), (2, m2), (3, m3)):
        msg[...] = w[:, y ^ d].astype(F32).reshape(8 * ROWS, COLS).astype(BF16)
    mine = a[:, y].astype(F32).reshape(8 * ROWS, COLS)
    a_y[...] = mine
    own[...] = mine - w[:, y].astype(F32).reshape(8 * ROWS, COLS)
    mx[...] = jnp.broadcast_to(m, TOP)


def y_kernel(ix, own, a_y, g1, g2, g3, h, own4, s):
    lo = ix[2]
    mine = a_y[...]
    s[...] = own[...] + sum(mine - g[...].astype(F32) for g in (g1, g2, g3))

    def blocks(k):
        return [s[pl.ds((4 * b + k) * ROWS, ROWS)] for b in range(2)]

    h[...] = jnp.concatenate(blocks(lo ^ 1) + blocks(lo ^ 3)).astype(BF16)
    own4[...] = jnp.concatenate(blocks(lo) + blocks(lo ^ 2))


def near_kernel(ix, own4, g, h, own2):
    s = own4[...] + g[...].astype(F32)
    h[...] = s[2 * ROWS :].astype(BF16)
    own2[...] = s[: 2 * ROWS]


def lo_kernel(ix, own2, mom, h, mx, mr, q, p_own, mx2, s):
    hi = ix[1]
    m = jnp.maximum(mx[0:1], mr[0:1])
    s[...] = own2[...] + h[...].astype(F32)
    here = pl.ds(hi * ROWS, ROWS)
    p_own[...] = s[here]
    s[here] = s[here] + MOMENTUM_GAIN * mom[...]
    put(q, s[...], m)
    mx2[...] = jnp.broadcast_to(m, TOP)


def hi_kernel(ix, q, p_own, mom, a_y, mx, g, fresh, mom_new, mx2, s):
    hi, lo = ix[1], ix[2]
    m = jnp.maximum(mx[0:1], untail(g, 2 * ROWS))
    s[...] = g[0 : 2 * ROWS].astype(F32)
    total = q[0 : 2 * ROWS].astype(F32) + s[...]
    summed = p_own[...] + s[pl.ds(hi * ROWS, ROWS)]
    mom_new[...] = OUTER_MOMENTUM * mom[...] + summed * (1.0 / N_REPLICA)
    rows = jnp.concatenate([a_y[pl.ds((4 * b + lo) * ROWS, ROWS)] for b in range(2)])
    put(fresh, rows - STEP_GAIN * total, m)
    mx2[...] = jnp.broadcast_to(m, TOP)


def eight_kernel(ix, f0, f1, f2, f3, mx, eight, mx2, s):
    lo = ix[2]
    m = mx[0:1]
    for d, ref in enumerate((f0, f1, f2, f3)):
        x = ref[0 : 2 * ROWS].astype(F32)
        for b in range(2):
            s[pl.ds((4 * b + (lo ^ d)) * ROWS, ROWS)] = x[b * ROWS : (b + 1) * ROWS]
        if d > 0:
            m = jnp.maximum(m, untail(ref, 2 * ROWS))
    put(eight, s[...], m)
    mx2[...] = jnp.broadcast_to(m, TOP)


def out_kernel(ix, e0, e1, e2, e3, mx, out, scale):
    y = ix[0]
    n = 8 * ROWS
    m = mx[0:1]
    for d, e in enumerate((e0, e1, e2, e3)):
        out[:, y ^ d] = e[0:n].astype(F32).reshape(8, ROWS, COLS).astype(BF16)
        if d > 0:
            m = jnp.maximum(m, untail(e, n))
    scale[...] = jnp.broadcast_to(m, TOP) + EPSILON


def pair_kernel(ix, a, b, mx, theirs, mine, mx2):
    t = ix[4]
    m = jnp.maximum(mx[0:1], untail(b, 2 * TOK))
    for i, ref in enumerate((a, b)):
        at = slice(i * TOK, (i + 1) * TOK)
        theirs[at] = ref[pl.ds(pl.multiple_of((1 - t) * TOK, 16), TOK)]
        mine[at] = ref[pl.ds(pl.multiple_of(t * TOK, 16), TOK)]
    theirs[2 * TOK :] = tail(m)
    mx2[...] = jnp.broadcast_to(m, TOP)


def core_kernel(ix, mine, g, mx, both, mx2):
    both[0 : 2 * TOK] = mine[...]
    both[2 * TOK :] = g[0 : 2 * TOK]
    mx2[...] = jnp.broadcast_to(jnp.maximum(mx[0:1], untail(g, 2 * TOK))[:, :128], (8, 128))


def quad_kernel(ix, a, b, quad):
    n = 2 * TOK
    for k in range(2):
        quad[2 * k * n : (2 * k + 1) * n] = a[k * n : (k + 1) * n]
        quad[(2 * k + 1) * n : (2 * k + 2) * n] = b[k * n : (k + 1) * n]


def product_kernel(place, a, wa, wb, *rest):
    out, buf, sem = rest[-3:]
    dims = (((1,), (1,)), ((), ()))
    n = 4 * TOK
    copies = []
    for j in range(wa.shape[0] // COLS):
        at = slice(j * COLS, (j + 1) * COLS)
        x = lax.dot_general(a[0:n], wa[at], dims, preferred_element_type=F32)
        x += lax.dot_general(a[n:], wb[at], dims, preferred_element_type=F32)
        buf[j] = x.astype(BF16)
        for i in range(4):
            src = buf.at[j, pl.ds(i * TOK, TOK)]
            copy = pltpu.make_async_copy(src, out.at[place[i], :, pl.ds(j * COLS, COLS)], sem.at[j, i])
            copy.start()
            copies.append(copy)
    for copy in copies:
        copy.wait()


def product(place, rows, w, w_other, prod=None):
    width = w.shape[0]
    blocks = width // COLS
    args = [place, rows, w, w_other] + ([] if prod is None else [prod])
    return pl.pallas_call(
        product_kernel,
        in_specs=[SMEM, VMEM, VMEM, VMEM] + [pl.BlockSpec(memory_space=pl.ANY)] * (len(args) - 4),
        out_specs=pl.BlockSpec(memory_space=pl.ANY),
        out_shape=jax.ShapeDtypeStruct((8, TOK, width), BF16),
        scratch_shapes=[
            pltpu.VMEM((blocks, 4 * TOK, COLS), BF16),
            pltpu.SemaphoreType.DMA((blocks, 4)),
        ],
        input_output_aliases={} if prod is None else {4: 0},
        compiler_params=pltpu.CompilerParams(vmem_limit_bytes=24 * 1024 * 1024),
        cost_estimate=pl.CostEstimate(flops=8 * TOK * width * 2 * COLS, bytes_accessed=3_500_000, transcendentals=0),
    )(*args)


def body(w_local, anchor, momentum, key_grad):
    r = lax.axis_index("replica")
    f = lax.axis_index("fsdp")
    t = lax.axis_index("tensor")
    ix = jnp.stack([r & 3, r >> 4, (r >> 2) & 3, f, t])
    w = w_local[0]
    mom = momentum[0, 0]
    top = (TOP, F32)

    def bf(n):
        return ((n, COLS), BF16)

    def fl(n):
        return ((n, COLS), F32)

    w_other = swap(w, "tensor", 1)
    four = (8, 4, ROWS, COLS)
    m1, m2, m3, own, a_y, kgm, mx = call(
        start_kernel,
        [bf(320)] * 3 + [fl(320)] * 2 + [bf(304), top],
        (ix, w.reshape(four), anchor.reshape(four), key_grad[0]),
    )
    kg_far = swap(kgm, "fsdp", 4)
    g2, g1, g3 = (swap(m, "replica", d) for d, m in ((2, m2), (1, m1), (3, m3)))
    h, own4 = call(y_kernel, [bf(160), fl(160)], (ix, own, a_y, g1, g2, g3), [fl(320)])
    theirs, kg_mine, mx = call(pair_kernel, [bf(304), bf(288), top], (ix, kgm, kg_far, mx))
    h = swap(h, "replica", 4)
    kg_core = swap(theirs, "tensor", 1)
    h, own2 = call(near_kernel, [bf(80), fl(80)], (ix, own4, h))
    h = swap(h, "replica", 8)
    both, ms = call(core_kernel, [bf(576), ((8, 128), F32)], (ix, kg_mine, kg_core, mx))
    ms = jnp.maximum(ms, swap(ms, "fsdp", 1))
    mr = swap(ms, "fsdp", 3)
    wide = [jnp.concatenate([m, m], axis=1) for m in (ms, mr)]
    q, p_own, mx = call(lo_kernel, [bf(96), fl(40), top], (ix, own2, mom, h, *wide), [fl(80)])
    g = swap(q, "replica", 16)
    kg_x = swap(tie(both, q), "fsdp", 1)
    fresh, mom_new, mx = call(hi_kernel, [bf(96), fl(40), top], (ix, q, p_own, mom, a_y, mx, g), [fl(80)], 6.0)
    f3, f2, f1 = (swap(fresh, "replica", 4 * d) for d in (3, 2, 1))
    quad = call(quad_kernel, [bf(1152)], (ix, both, tie(kg_x, (f1, f2, f3))))[0]
    more = swap(quad, "fsdp", 3)
    place = jnp.array([0, 4, 1, 5, 3, 7, 2, 6], jnp.int32) ^ f
    prod = product(place[:4], quad, w, w_other)
    eight, mx = call(eight_kernel, [bf(336), top], (ix, fresh, f1, f2, f3, mx), [fl(320)])
    e2, e1, e3 = (swap(eight, "replica", d) for d in (2, 1, 3))
    prod = product(place[4:], tie(more, eight), w, w_other, prod)
    new_weights, scale = call(out_kernel, [(four, BF16), top], (ix, eight, e1, tie(e2, prod), e3, mx))
    return new_weights.reshape(anchor.shape), mom_new[None, None], prod[None], scale[0, :1]


def solution(mesh):
    return jax.shard_map(
        body,
        mesh=mesh,
        in_specs=(
            P("replica", "fsdp", "tensor"),
            P("fsdp", "tensor"),
            P("fsdp", "replica", None, "tensor"),
            P("replica", "fsdp", "tensor"),
        ),
        out_specs=(
            P("fsdp", "tensor"),
            P("fsdp", "replica", None, "tensor"),
            P("replica", None, "tensor", "fsdp"),
            P(),
        ),
        check_vma=False,
    )
```

```python
import jax
import jax.numpy as jnp
from jax import lax
from jax.experimental import pallas as pl
from jax.experimental.pallas import tpu as pltpu
from jax.sharding import PartitionSpec as P

OUTER_MOMENTUM = 0.9
OUTER_RATE = 0.7
EPSILON = 1e-06
N_REPLICA = 32
STEP_GAIN = OUTER_RATE * (1.0 + OUTER_MOMENTUM) / N_REPLICA
MOMENTUM_GAIN = OUTER_MOMENTUM * OUTER_MOMENTUM * N_REPLICA / (1.0 + OUTER_MOMENTUM)
F32, BF16 = jnp.float32, jnp.bfloat16
ROWS, COLS, TAIL, TOK = 40, 256, 16, 144
TOP = (8, COLS)
VMEM = pl.BlockSpec(memory_space=pltpu.VMEM)
SMEM = pl.BlockSpec(memory_space=pltpu.SMEM)


def swap(x, axis, bit):
    n = lax.axis_size(axis)
    return lax.ppermute(x, axis, [(i, i ^ bit) for i in range(n)])


def tie(x, dep):
    return lax.optimization_barrier((x, dep))[0]


def call(kernel, outs, args, scratch=(), micros=0.5):
    return pl.pallas_call(
        kernel,
        out_shape=[jax.ShapeDtypeStruct(s, d) for s, d in outs],
        in_specs=[SMEM] + [VMEM] * (len(args) - 1),
        out_specs=[VMEM] * len(outs),
        scratch_shapes=[pltpu.VMEM(s, d) for s, d in scratch],
        compiler_params=pltpu.CompilerParams(vmem_limit_bytes=24 * 1024 * 1024),
        cost_estimate=pl.CostEstimate(flops=int(micros * 1e9), bytes_accessed=0, transcendentals=0),
    )(*args)


def tail(m):
    a = m.astype(BF16).astype(F32)
    b = (m - a).astype(BF16).astype(F32)
    c = m - a - b
    row = lax.broadcasted_iota(jnp.int32, (TAIL, COLS), 0)
    return jnp.where(row == 0, a, jnp.where(row == 1, b, c)).astype(BF16)


def untail(ref, rows):
    p = ref[rows : rows + TAIL].astype(F32)
    return p[0:1] + p[1:2] + p[2:3]


def put(msg, rows, m):
    n = rows.shape[0]
    msg[0:n] = rows.astype(BF16)
    msg[n : n + TAIL] = tail(m)


def start_kernel(ix, w, a, kg, m1, m2, m3, own, a_y, kgm, mx):
    y = ix[0]
    top = jnp.zeros(TOP, F32)
    for i in range(8):
        d = jnp.abs(a[i].astype(F32) - w[i].astype(F32)).reshape(-1, 8, COLS)
        top = jnp.maximum(top, jnp.max(d, axis=0))
    m = jnp.broadcast_to(jnp.max(top), (1, COLS))
    kgm[0 : 2 * TOK] = kg[...]
    kgm[2 * TOK :] = tail(m)
    for d, msg in ((1, m1), (2, m2), (3, m3)):
        msg[...] = w[:, y ^ d].astype(F32).reshape(8 * ROWS, COLS).astype(BF16)
    mine = a[:, y].astype(F32).reshape(8 * ROWS, COLS)
    a_y[...] = mine
    own[...] = mine - w[:, y].astype(F32).reshape(8 * ROWS, COLS)
    mx[...] = jnp.broadcast_to(m, TOP)


def y_kernel(ix, own, a_y, g1, g2, g3, h, own4, s):
    lo = ix[2]
    mine = a_y[...]
    s[...] = own[...] + sum(mine - g[...].astype(F32) for g in (g1, g2, g3))

    def blocks(k):
        return [s[pl.ds((4 * b + k) * ROWS, ROWS)] for b in range(2)]

    h[...] = jnp.concatenate(blocks(lo ^ 1) + blocks(lo ^ 3)).astype(BF16)
    own4[...] = jnp.concatenate(blocks(lo) + blocks(lo ^ 2))


def near_kernel(ix, own4, g, h, own2):
    s = own4[...] + g[...].astype(F32)
    h[...] = s[2 * ROWS :].astype(BF16)
    own2[...] = s[: 2 * ROWS]


def lo_kernel(ix, own2, mom, h, mx, mr, q, p_own, mx2, s):
    hi = ix[1]
    m = jnp.maximum(mx[0:1], mr[0:1])
    s[...] = own2[...] + h[...].astype(F32)
    here = pl.ds(hi * ROWS, ROWS)
    p_own[...] = s[here]
    s[here] = s[here] + MOMENTUM_GAIN * mom[...]
    put(q, s[...], m)
    mx2[...] = jnp.broadcast_to(m, TOP)


def hi_kernel(ix, q, p_own, mom, a_y, mx, g, fresh, mom_new, mx2, s):
    hi, lo = ix[1], ix[2]
    m = jnp.maximum(mx[0:1], untail(g, 2 * ROWS))
    s[...] = g[0 : 2 * ROWS].astype(F32)
    total = q[0 : 2 * ROWS].astype(F32) + s[...]
    summed = p_own[...] + s[pl.ds(hi * ROWS, ROWS)]
    mom_new[...] = OUTER_MOMENTUM * mom[...] + summed * (1.0 / N_REPLICA)
    rows = jnp.concatenate([a_y[pl.ds((4 * b + lo) * ROWS, ROWS)] for b in range(2)])
    put(fresh, rows - STEP_GAIN * total, m)
    mx2[...] = jnp.broadcast_to(m, TOP)


def eight_kernel(ix, f0, f1, f2, f3, mx, eight, mx2, s):
    lo = ix[2]
    m = mx[0:1]
    for d, ref in enumerate((f0, f1, f2, f3)):
        x = ref[0 : 2 * ROWS].astype(F32)
        for b in range(2):
            s[pl.ds((4 * b + (lo ^ d)) * ROWS, ROWS)] = x[b * ROWS : (b + 1) * ROWS]
        if d > 0:
            m = jnp.maximum(m, untail(ref, 2 * ROWS))
    put(eight, s[...], m)
    mx2[...] = jnp.broadcast_to(m, TOP)


def out_kernel(ix, e0, e1, e2, e3, mx, out, scale):
    y = ix[0]
    n = 8 * ROWS
    m = mx[0:1]
    for d, e in enumerate((e0, e1, e2, e3)):
        out[:, y ^ d] = e[0:n].astype(F32).reshape(8, ROWS, COLS).astype(BF16)
        if d > 0:
            m = jnp.maximum(m, untail(e, n))
    scale[...] = m[:, 0:1] + EPSILON


def pair_kernel(ix, a, b, mx, theirs, mine, mx2):
    t = ix[4]
    m = jnp.maximum(mx[0:1], untail(b, 2 * TOK))
    for i, ref in enumerate((a, b)):
        at = slice(i * TOK, (i + 1) * TOK)
        theirs[at] = ref[pl.ds(pl.multiple_of((1 - t) * TOK, 16), TOK)]
        mine[at] = ref[pl.ds(pl.multiple_of(t * TOK, 16), TOK)]
    theirs[2 * TOK :] = tail(m)
    mx2[...] = jnp.broadcast_to(m, TOP)


def core_kernel(ix, mine, g, mx, both, mx2):
    both[0 : 2 * TOK] = mine[...]
    both[2 * TOK :] = g[0 : 2 * TOK]
    mx2[...] = jnp.broadcast_to(jnp.maximum(mx[0:1], untail(g, 2 * TOK))[:, :128], (8, 128))


def quad_kernel(ix, a, b, quad):
    n = 2 * TOK
    for k in range(2):
        quad[2 * k * n : (2 * k + 1) * n] = a[k * n : (k + 1) * n]
        quad[(2 * k + 1) * n : (2 * k + 2) * n] = b[k * n : (k + 1) * n]


def product_kernel(place, a, wa, wb, *rest):
    out, buf, sem = rest[-3:]
    dims = (((1,), (1,)), ((), ()))
    n = 4 * TOK
    copies = []
    for j in range(wa.shape[0] // COLS):
        at = slice(j * COLS, (j + 1) * COLS)
        x = lax.dot_general(a[0:n], wa[at], dims, preferred_element_type=F32)
        x += lax.dot_general(a[n:], wb[at], dims, preferred_element_type=F32)
        buf[j] = x.astype(BF16)
        for i in range(4):
            src = buf.at[j, pl.ds(i * TOK, TOK)]
            copy = pltpu.make_async_copy(src, out.at[place[i], :, pl.ds(j * COLS, COLS)], sem.at[j, i])
            copy.start()
            copies.append(copy)
    for copy in copies:
        copy.wait()


def product(place, rows, w, w_other, prod=None):
    width = w.shape[0]
    blocks = width // COLS
    args = [place, rows, w, w_other] + ([] if prod is None else [prod])
    return pl.pallas_call(
        product_kernel,
        in_specs=[SMEM, VMEM, VMEM, VMEM] + [pl.BlockSpec(memory_space=pl.ANY)] * (len(args) - 4),
        out_specs=pl.BlockSpec(memory_space=pl.ANY),
        out_shape=jax.ShapeDtypeStruct((8, TOK, width), BF16),
        scratch_shapes=[
            pltpu.VMEM((blocks, 4 * TOK, COLS), BF16),
            pltpu.SemaphoreType.DMA((blocks, 4)),
        ],
        input_output_aliases={} if prod is None else {4: 0},
        compiler_params=pltpu.CompilerParams(vmem_limit_bytes=24 * 1024 * 1024),
        cost_estimate=pl.CostEstimate(flops=8 * TOK * width * 2 * COLS, bytes_accessed=3_500_000, transcendentals=0),
    )(*args)


def body(w_local, anchor, momentum, key_grad):
    r = lax.axis_index("replica")
    f = lax.axis_index("fsdp")
    t = lax.axis_index("tensor")
    ix = jnp.stack([r & 3, r >> 4, (r >> 2) & 3, f, t])
    w = w_local[0]
    mom = momentum[0, 0]
    top = (TOP, F32)

    def bf(n):
        return ((n, COLS), BF16)

    def fl(n):
        return ((n, COLS), F32)

    w_other = swap(w, "tensor", 1)
    four = (8, 4, ROWS, COLS)
    m1, m2, m3, own, a_y, kgm, mx = call(
        start_kernel,
        [bf(320)] * 3 + [fl(320)] * 2 + [bf(304), top],
        (ix, w.reshape(four), anchor.reshape(four), key_grad[0]),
    )
    kg_far = swap(kgm, "fsdp", 4)
    g2, g1, g3 = (swap(m, "replica", d) for d, m in ((2, m2), (1, m1), (3, m3)))
    h, own4 = call(y_kernel, [bf(160), fl(160)], (ix, own, a_y, g1, g2, g3), [fl(320)])
    theirs, kg_mine, mx = call(pair_kernel, [bf(304), bf(288), top], (ix, kgm, kg_far, mx))
    h = swap(h, "replica", 4)
    kg_core = swap(theirs, "tensor", 1)
    h, own2 = call(near_kernel, [bf(80), fl(80)], (ix, own4, h))
    h = swap(h, "replica", 8)
    both, ms = call(core_kernel, [bf(576), ((8, 128), F32)], (ix, kg_mine, kg_core, mx))
    ms = jnp.maximum(ms, swap(ms, "fsdp", 1))
    mr = swap(ms, "fsdp", 3)
    kg_x = swap(tie(both, (h, ms)), "fsdp", 1)
    wide = [jnp.concatenate([m, m], axis=1) for m in (ms, mr)]
    q, p_own, mx = call(lo_kernel, [bf(96), fl(40), top], (ix, own2, mom, h, *wide), [fl(80)])
    g = swap(q, "replica", 16)
    fresh, mom_new, mx = call(hi_kernel, [bf(96), fl(40), top], (ix, q, p_own, mom, a_y, mx, g), [fl(80)], 14.0)
    f3, f2, f1 = (swap(fresh, "replica", 4 * d) for d in (3, 2, 1))
    quad = call(quad_kernel, [bf(1152)], (ix, both, tie(kg_x, q)))[0]
    more = swap(quad, "fsdp", 3)
    place = jnp.array([0, 4, 1, 5, 3, 7, 2, 6], jnp.int32) ^ f
    prod = product(place[:4], quad, w, w_other)
    eight, mx = call(eight_kernel, [bf(336), top], (ix, fresh, f1, f2, tie(f3, prod), mx), [fl(320)])
    e2, e1, e3 = (swap(eight, "replica", d) for d in (2, 1, 3))
    prod = product(place[4:], tie(more, eight), w, w_other, prod)
    new_weights, scale = call(out_kernel, [(four, BF16), ((1, 1), F32)], (ix, eight, e1, tie(e2, prod), e3, mx))
    return new_weights.reshape(anchor.shape), mom_new[None, None], prod[None], scale.reshape(1)


def solution(mesh):
    return jax.shard_map(
        body,
        mesh=mesh,
        in_specs=(
            P("replica", "fsdp", "tensor"),
            P("fsdp", "tensor"),
            P("fsdp", "replica", None, "tensor"),
            P("replica", "fsdp", "tensor"),
        ),
        out_specs=(
            P("fsdp", "tensor"),
            P("fsdp", "replica", None, "tensor"),
            P("replica", None, "tensor", "fsdp"),
            P(),
        ),
        check_vma=False,
    )
```

```python
import jax
import jax.numpy as jnp
from jax import lax
from jax.experimental import pallas as pl
from jax.experimental.pallas import tpu as pltpu
from jax.sharding import PartitionSpec as P

OUTER_MOMENTUM = 0.9
OUTER_RATE = 0.7
EPSILON = 1e-06
N_REPLICA = 32
STEP_GAIN = OUTER_RATE * (1.0 + OUTER_MOMENTUM) / N_REPLICA
MOMENTUM_GAIN = OUTER_MOMENTUM * OUTER_MOMENTUM * N_REPLICA / (1.0 + OUTER_MOMENTUM)
F32, BF16 = jnp.float32, jnp.bfloat16
ROWS, COLS, TAIL, TOK = 40, 256, 16, 144
TOP = (8, COLS)
VMEM = pl.BlockSpec(memory_space=pltpu.VMEM)
SMEM = pl.BlockSpec(memory_space=pltpu.SMEM)


def swap(x, axis, bit):
    n = lax.axis_size(axis)
    return lax.ppermute(x, axis, [(i, i ^ bit) for i in range(n)])


def tie(x, dep):
    return lax.optimization_barrier((x, dep))[0]


def call(kernel, outs, args, scratch=(), micros=0.5):
    return pl.pallas_call(
        kernel,
        out_shape=[jax.ShapeDtypeStruct(s, d) for s, d in outs],
        in_specs=[SMEM] + [VMEM] * (len(args) - 1),
        out_specs=[VMEM] * len(outs),
        scratch_shapes=[pltpu.VMEM(s, d) for s, d in scratch],
        compiler_params=pltpu.CompilerParams(vmem_limit_bytes=24 * 1024 * 1024),
        cost_estimate=pl.CostEstimate(flops=int(micros * 1e9), bytes_accessed=0, transcendentals=0),
    )(*args)


def tail(m):
    a = m.astype(BF16).astype(F32)
    b = (m - a).astype(BF16).astype(F32)
    c = m - a - b
    row = lax.broadcasted_iota(jnp.int32, (TAIL, COLS), 0)
    return jnp.where(row == 0, a, jnp.where(row == 1, b, c)).astype(BF16)


def untail(ref, rows):
    p = ref[rows : rows + TAIL].astype(F32)
    return p[0:1] + p[1:2] + p[2:3]


def put(msg, rows, m):
    n = rows.shape[0]
    msg[0:n] = rows.astype(BF16)
    msg[n : n + TAIL] = tail(m)


def start_kernel(ix, w, a, kg, m1, m2, m3, own, a_y, kgm, mx):
    y = ix[0]
    top = jnp.zeros(TOP, F32)
    for i in range(8):
        d = jnp.abs(a[i].astype(F32) - w[i].astype(F32)).reshape(-1, 8, COLS)
        top = jnp.maximum(top, jnp.max(d, axis=0))
    m = jnp.broadcast_to(jnp.max(top), (1, COLS))
    kgm[0 : 2 * TOK] = kg[...]
    kgm[2 * TOK :] = tail(m)
    for d, msg in ((1, m1), (2, m2), (3, m3)):
        msg[...] = w[:, y ^ d].astype(F32).reshape(8 * ROWS, COLS).astype(BF16)
    mine = a[:, y].astype(F32).reshape(8 * ROWS, COLS)
    a_y[...] = mine
    own[...] = mine - w[:, y].astype(F32).reshape(8 * ROWS, COLS)
    mx[...] = jnp.broadcast_to(m, TOP)


def y_kernel(ix, own, a_y, g1, g2, g3, h, own4, s):
    lo = ix[2]
    mine = a_y[...]
    s[...] = own[...] + sum(mine - g[...].astype(F32) for g in (g1, g2, g3))

    def blocks(k):
        return [s[pl.ds((4 * b + k) * ROWS, ROWS)] for b in range(2)]

    h[...] = jnp.concatenate(blocks(lo ^ 1) + blocks(lo ^ 3)).astype(BF16)
    own4[...] = jnp.concatenate(blocks(lo) + blocks(lo ^ 2))


def near_kernel(ix, own4, g, h, own2):
    s = own4[...] + g[...].astype(F32)
    h[...] = s[2 * ROWS :].astype(BF16)
    own2[...] = s[: 2 * ROWS]


def lo_kernel(ix, own2, mom, h, mx, mr, q, p_own, mx2, s):
    hi = ix[1]
    m = jnp.maximum(mx[0:1], mr[0:1])
    s[...] = own2[...] + h[...].astype(F32)
    here = pl.ds(hi * ROWS, ROWS)
    p_own[...] = s[here]
    s[here] = s[here] + MOMENTUM_GAIN * mom[...]
    put(q, s[...], m)
    mx2[...] = jnp.broadcast_to(m, TOP)


def hi_kernel(ix, q, p_own, mom, a_y, mx, g, fresh, mom_new, mx2, s):
    hi, lo = ix[1], ix[2]
    m = jnp.maximum(mx[0:1], untail(g, 2 * ROWS))
    s[...] = g[0 : 2 * ROWS].astype(F32)
    total = q[0 : 2 * ROWS].astype(F32) + s[...]
    summed = p_own[...] + s[pl.ds(hi * ROWS, ROWS)]
    mom_new[...] = OUTER_MOMENTUM * mom[...] + summed * (1.0 / N_REPLICA)
    rows = jnp.concatenate([a_y[pl.ds((4 * b + lo) * ROWS, ROWS)] for b in range(2)])
    put(fresh, rows - STEP_GAIN * total, m)
    mx2[...] = jnp.broadcast_to(m, TOP)


def eight_kernel(ix, f0, f1, f2, f3, mx, eight, mx2, s):
    lo = ix[2]
    m = mx[0:1]
    for d, ref in enumerate((f0, f1, f2, f3)):
        x = ref[0 : 2 * ROWS].astype(F32)
        for b in range(2):
            s[pl.ds((4 * b + (lo ^ d)) * ROWS, ROWS)] = x[b * ROWS : (b + 1) * ROWS]
        if d > 0:
            m = jnp.maximum(m, untail(ref, 2 * ROWS))
    put(eight, s[...], m)
    mx2[...] = jnp.broadcast_to(m, TOP)


def out_kernel(ix, e0, e1, e2, e3, mx, out, scale):
    y = ix[0]
    n = 8 * ROWS
    m = mx[0:1]
    for d, e in enumerate((e0, e1, e2, e3)):
        out[:, y ^ d] = e[0:n].astype(F32).reshape(8, ROWS, COLS).astype(BF16)
        if d > 0:
            m = jnp.maximum(m, untail(e, n))
    scale[...] = m[:, 0:1] + EPSILON


def pair_kernel(ix, a, b, mx, theirs, mine, mx2):
    t = ix[4]
    m = jnp.maximum(mx[0:1], untail(b, 2 * TOK))
    for i, ref in enumerate((a, b)):
        at = slice(i * TOK, (i + 1) * TOK)
        theirs[at] = ref[pl.ds(pl.multiple_of((1 - t) * TOK, 16), TOK)]
        mine[at] = ref[pl.ds(pl.multiple_of(t * TOK, 16), TOK)]
    theirs[2 * TOK :] = tail(m)
    mx2[...] = jnp.broadcast_to(m, TOP)


def core_kernel(ix, mine, g, mx, both, mx2):
    both[0 : 2 * TOK] = mine[...]
    both[2 * TOK :] = g[0 : 2 * TOK]
    mx2[...] = jnp.broadcast_to(jnp.maximum(mx[0:1], untail(g, 2 * TOK))[:, :128], (8, 128))


def quad_kernel(ix, a, b, quad):
    n = 2 * TOK
    for k in range(2):
        quad[2 * k * n : (2 * k + 1) * n] = a[k * n : (k + 1) * n]
        quad[(2 * k + 1) * n : (2 * k + 2) * n] = b[k * n : (k + 1) * n]


def product_kernel(place, a, wa, wb, *rest):
    out, buf, sem = rest[-3:]
    dims = (((1,), (1,)), ((), ()))
    n = 4 * TOK
    copies = []
    for j in range(wa.shape[0] // COLS):
        at = slice(j * COLS, (j + 1) * COLS)
        x = lax.dot_general(a[0:n], wa[at], dims, preferred_element_type=F32)
        x += lax.dot_general(a[n:], wb[at], dims, preferred_element_type=F32)
        buf[j] = x.astype(BF16)
        for i in range(4):
            src = buf.at[j, pl.ds(i * TOK, TOK)]
            copy = pltpu.make_async_copy(src, out.at[place[i], :, pl.ds(j * COLS, COLS)], sem.at[j, i])
            copy.start()
            copies.append(copy)
    for copy in copies:
        copy.wait()


def product(place, rows, w, w_other, prod=None):
    width = w.shape[0]
    blocks = width // COLS
    args = [place, rows, w, w_other] + ([] if prod is None else [prod])
    return pl.pallas_call(
        product_kernel,
        in_specs=[SMEM, VMEM, VMEM, VMEM] + [pl.BlockSpec(memory_space=pl.ANY)] * (len(args) - 4),
        out_specs=pl.BlockSpec(memory_space=pl.ANY),
        out_shape=jax.ShapeDtypeStruct((8, TOK, width), BF16),
        scratch_shapes=[
            pltpu.VMEM((blocks, 4 * TOK, COLS), BF16),
            pltpu.SemaphoreType.DMA((blocks, 4)),
        ],
        input_output_aliases={} if prod is None else {4: 0},
        compiler_params=pltpu.CompilerParams(vmem_limit_bytes=24 * 1024 * 1024),
        cost_estimate=pl.CostEstimate(flops=8 * TOK * width * 2 * COLS, bytes_accessed=3_500_000, transcendentals=0),
    )(*args)


def body(w_local, anchor, momentum, key_grad):
    r = lax.axis_index("replica")
    f = lax.axis_index("fsdp")
    t = lax.axis_index("tensor")
    ix = jnp.stack([r & 3, r >> 4, (r >> 2) & 3, f, t])
    w = w_local[0]
    mom = momentum[0, 0]
    top = (TOP, F32)

    def bf(n):
        return ((n, COLS), BF16)

    def fl(n):
        return ((n, COLS), F32)

    w_other = swap(w, "tensor", 1)
    four = (8, 4, ROWS, COLS)
    m1, m2, m3, own, a_y, kgm, mx = call(
        start_kernel,
        [bf(320)] * 3 + [fl(320)] * 2 + [bf(304), top],
        (ix, w.reshape(four), anchor.reshape(four), key_grad[0]),
    )
    kg_far = swap(kgm, "fsdp", 4)
    g2, g1, g3 = (swap(m, "replica", d) for d, m in ((2, m2), (1, m1), (3, m3)))
    h, own4 = call(y_kernel, [bf(160), fl(160)], (ix, own, a_y, g1, g2, g3), [fl(320)])
    theirs, kg_mine, mx = call(pair_kernel, [bf(304), bf(288), top], (ix, kgm, kg_far, mx))
    h = swap(h, "replica", 4)
    kg_core = swap(theirs, "tensor", 1)
    h, own2 = call(near_kernel, [bf(80), fl(80)], (ix, own4, h))
    h = swap(h, "replica", 8)
    both, ms = call(core_kernel, [bf(576), ((8, 128), F32)], (ix, kg_mine, kg_core, mx))
    ms = jnp.maximum(ms, swap(ms, "fsdp", 1))
    mr = swap(ms, "fsdp", 3)
    kg_x = swap(tie(both, (h, ms)), "fsdp", 1)
    wide = [jnp.concatenate([m, m], axis=1) for m in (ms, mr)]
    q, p_own, mx = call(lo_kernel, [bf(96), fl(40), top], (ix, own2, mom, h, *wide), [fl(80)])
    g = swap(q, "replica", 16)
    fresh, mom_new, mx = call(hi_kernel, [bf(96), fl(40), top], (ix, q, p_own, mom, a_y, mx, g), [fl(80)], 14.0)
    f3, f2, f1 = (swap(fresh, "replica", 4 * d) for d in (3, 2, 1))
    quad = call(quad_kernel, [bf(1152)], (ix, both, tie(kg_x, q)))[0]
    more = swap(quad, "fsdp", 3)
    place = jnp.array([0, 4, 1, 5, 3, 7, 2, 6], jnp.int32) ^ f
    prod = product(place[:4], quad, w, w_other)
    eight, mx = call(eight_kernel, [bf(336), top], (ix, fresh, f1, f2, tie(f3, prod), mx), [fl(320)])
    e2, e1, e3 = (swap(eight, "replica", d) for d in (2, 1, 3))
    prod = product(place[4:], tie(more, eight), w, w_other, prod)
    new_weights, scale = call(out_kernel, [(four, BF16), ((1, 1), F32)], (ix, eight, e1, e2, tie(e3, prod), mx))
    return new_weights.reshape(anchor.shape), mom_new[None, None], prod[None], scale.reshape(1)


def solution(mesh):
    return jax.shard_map(
        body,
        mesh=mesh,
        in_specs=(
            P("replica", "fsdp", "tensor"),
            P("fsdp", "tensor"),
            P("fsdp", "replica", None, "tensor"),
            P("replica", "fsdp", "tensor"),
        ),
        out_specs=(
            P("fsdp", "tensor"),
            P("fsdp", "replica", None, "tensor"),
            P("replica", None, "tensor", "fsdp"),
            P(),
        ),
        check_vma=False,
    )
```

```python
import jax
import jax.numpy as jnp
from jax import lax
from jax.experimental import pallas as pl
from jax.experimental.pallas import tpu as pltpu
from jax.sharding import PartitionSpec as P

OUTER_MOMENTUM = 0.9
OUTER_RATE = 0.7
EPSILON = 1e-06
N_REPLICA = 32
STEP_GAIN = OUTER_RATE * (1.0 + OUTER_MOMENTUM) / N_REPLICA
MOMENTUM_GAIN = OUTER_MOMENTUM * OUTER_MOMENTUM * N_REPLICA / (1.0 + OUTER_MOMENTUM)
F32, BF16 = jnp.float32, jnp.bfloat16
ROWS, COLS, TAIL, TOK = 40, 256, 16, 144
TOP = (8, COLS)
VMEM = pl.BlockSpec(memory_space=pltpu.VMEM)
SMEM = pl.BlockSpec(memory_space=pltpu.SMEM)


def swap(x, axis, bit):
    n = lax.axis_size(axis)
    return lax.ppermute(x, axis, [(i, i ^ bit) for i in range(n)])


def tie(x, dep):
    return lax.optimization_barrier((x, dep))[0]


def call(kernel, outs, args, scratch=(), micros=0.5):
    return pl.pallas_call(
        kernel,
        out_shape=[jax.ShapeDtypeStruct(s, d) for s, d in outs],
        in_specs=[SMEM] + [VMEM] * (len(args) - 1),
        out_specs=[VMEM] * len(outs),
        scratch_shapes=[pltpu.VMEM(s, d) for s, d in scratch],
        compiler_params=pltpu.CompilerParams(vmem_limit_bytes=24 * 1024 * 1024),
        cost_estimate=pl.CostEstimate(flops=int(micros * 1e9), bytes_accessed=0, transcendentals=0),
    )(*args)


def tail(m):
    a = m.astype(BF16).astype(F32)
    b = (m - a).astype(BF16).astype(F32)
    c = m - a - b
    row = lax.broadcasted_iota(jnp.int32, (TAIL, COLS), 0)
    return jnp.where(row == 0, a, jnp.where(row == 1, b, c)).astype(BF16)


def untail(ref, rows):
    p = ref[rows : rows + TAIL].astype(F32)
    return p[0:1] + p[1:2] + p[2:3]


def put(msg, rows, m):
    n = rows.shape[0]
    msg[0:n] = rows.astype(BF16)
    msg[n : n + TAIL] = tail(m)


def start_kernel(ix, w, a, kg, m1, m2, m3, own, a_y, kgm, mx):
    y = ix[0]
    top = jnp.zeros(TOP, F32)
    for i in range(8):
        d = jnp.abs(a[i].astype(F32) - w[i].astype(F32)).reshape(-1, 8, COLS)
        top = jnp.maximum(top, jnp.max(d, axis=0))
    m = jnp.broadcast_to(jnp.max(top), (1, COLS))
    kgm[0 : 2 * TOK] = kg[...]
    kgm[2 * TOK :] = tail(m)
    for d, msg in ((1, m1), (2, m2), (3, m3)):
        msg[...] = w[:, y ^ d].astype(F32).reshape(8 * ROWS, COLS).astype(BF16)
    mine = a[:, y].astype(F32).reshape(8 * ROWS, COLS)
    a_y[...] = mine
    own[...] = mine - w[:, y].astype(F32).reshape(8 * ROWS, COLS)
    mx[...] = jnp.broadcast_to(m, TOP)


def y_kernel(ix, own, a_y, g1, g2, g3, h, own4, s):
    lo = ix[2]
    mine = a_y[...]
    s[...] = own[...] + sum(mine - g[...].astype(F32) for g in (g1, g2, g3))

    def blocks(k):
        return [s[pl.ds((4 * b + k) * ROWS, ROWS)] for b in range(2)]

    h[...] = jnp.concatenate(blocks(lo ^ 1) + blocks(lo ^ 3)).astype(BF16)
    own4[...] = jnp.concatenate(blocks(lo) + blocks(lo ^ 2))


def near_kernel(ix, own4, g, h, own2):
    s = own4[...] + g[...].astype(F32)
    h[...] = s[2 * ROWS :].astype(BF16)
    own2[...] = s[: 2 * ROWS]


def lo_kernel(ix, own2, mom, h, mx, mr, q, p_own, mx2, s):
    hi = ix[1]
    m = jnp.maximum(mx[0:1], mr[0:1])
    s[...] = own2[...] + h[...].astype(F32)
    here = pl.ds(hi * ROWS, ROWS)
    p_own[...] = s[here]
    s[here] = s[here] + MOMENTUM_GAIN * mom[...]
    put(q, s[...], m)
    mx2[...] = jnp.broadcast_to(m, TOP)


def hi_kernel(ix, q, p_own, mom, a_y, mx, g, fresh, mom_new, mx2, s):
    hi, lo = ix[1], ix[2]
    m = jnp.maximum(mx[0:1], untail(g, 2 * ROWS))
    s[...] = g[0 : 2 * ROWS].astype(F32)
    total = q[0 : 2 * ROWS].astype(F32) + s[...]
    summed = p_own[...] + s[pl.ds(hi * ROWS, ROWS)]
    mom_new[...] = OUTER_MOMENTUM * mom[...] + summed * (1.0 / N_REPLICA)
    rows = jnp.concatenate([a_y[pl.ds((4 * b + lo) * ROWS, ROWS)] for b in range(2)])
    put(fresh, rows - STEP_GAIN * total, m)
    mx2[...] = jnp.broadcast_to(m, TOP)


def eight_kernel(ix, f0, f1, f2, f3, mx, eight, mx2, s):
    lo = ix[2]
    m = mx[0:1]
    for d, ref in enumerate((f0, f1, f2, f3)):
        x = ref[0 : 2 * ROWS].astype(F32)
        for b in range(2):
            s[pl.ds((4 * b + (lo ^ d)) * ROWS, ROWS)] = x[b * ROWS : (b + 1) * ROWS]
        if d > 0:
            m = jnp.maximum(m, untail(ref, 2 * ROWS))
    put(eight, s[...], m)
    mx2[...] = jnp.broadcast_to(m, TOP)


def out_kernel(ix, e0, e1, e2, e3, mx, out, scale):
    y = ix[0]
    n = 8 * ROWS
    m = mx[0:1]
    for d, e in enumerate((e0, e1, e2, e3)):
        out[:, y ^ d] = e[0:n].astype(F32).reshape(8, ROWS, COLS).astype(BF16)
        if d > 0:
            m = jnp.maximum(m, untail(e, n))
    scale[...] = m[:, 0:1] + EPSILON


def pair_kernel(ix, a, b, mx, theirs, mine, mx2):
    t = ix[4]
    m = jnp.maximum(mx[0:1], untail(b, 2 * TOK))
    for i, ref in enumerate((a, b)):
        at = slice(i * TOK, (i + 1) * TOK)
        theirs[at] = ref[pl.ds(pl.multiple_of((1 - t) * TOK, 16), TOK)]
        mine[at] = ref[pl.ds(pl.multiple_of(t * TOK, 16), TOK)]
    theirs[2 * TOK :] = tail(m)
    mx2[...] = jnp.broadcast_to(m, TOP)


def core_kernel(ix, mine, g, mx, both, mx2):
    both[0 : 2 * TOK] = mine[...]
    both[2 * TOK :] = g[0 : 2 * TOK]
    mx2[...] = jnp.broadcast_to(jnp.maximum(mx[0:1], untail(g, 2 * TOK))[:, :128], (8, 128))


def quad_kernel(ix, a, b, quad):
    n = 2 * TOK
    for k in range(2):
        quad[2 * k * n : (2 * k + 1) * n] = a[k * n : (k + 1) * n]
        quad[(2 * k + 1) * n : (2 * k + 2) * n] = b[k * n : (k + 1) * n]


def product_kernel(place, a, wa, wb, *rest):
    out, buf, w, sem, w_sem = rest[-5:]
    dims = (((1,), (1,)), ((), ()))
    n = 4 * TOK
    copies = []
    loads = []
    for j in range(wa.shape[0] // COLS):
        rows = pl.ds(j * COLS, COLS)
        loads.append(pltpu.make_async_copy(wa.at[rows], w.at[rows], w_sem.at[j]))
        loads[-1].start()
    for j, load in enumerate(loads):
        at = slice(j * COLS, (j + 1) * COLS)
        x = lax.dot_general(a[n:], wb[at], dims, preferred_element_type=F32)
        load.wait()
        x += lax.dot_general(a[0:n], w[at], dims, preferred_element_type=F32)
        buf[j] = x.astype(BF16)
        for i in range(4):
            src = buf.at[j, pl.ds(i * TOK, TOK)]
            copy = pltpu.make_async_copy(src, out.at[place[i], :, pl.ds(j * COLS, COLS)], sem.at[j, i])
            copy.start()
            copies.append(copy)
    for copy in copies:
        copy.wait()


def product(place, rows, w, w_other, prod=None):
    width = w.shape[0]
    blocks = width // COLS
    args = [place, rows, w, w_other] + ([] if prod is None else [prod])
    return pl.pallas_call(
        product_kernel,
        in_specs=[SMEM, VMEM, pl.BlockSpec(memory_space=pl.ANY), VMEM] + [pl.BlockSpec(memory_space=pl.ANY)] * (len(args) - 4),
        out_specs=pl.BlockSpec(memory_space=pl.ANY),
        out_shape=jax.ShapeDtypeStruct((8, TOK, width), BF16),
        scratch_shapes=[
            pltpu.VMEM((blocks, 4 * TOK, COLS), BF16),
            pltpu.VMEM((width, COLS), BF16),
            pltpu.SemaphoreType.DMA((blocks, 4)),
            pltpu.SemaphoreType.DMA((blocks,)),
        ],
        input_output_aliases={} if prod is None else {4: 0},
        compiler_params=pltpu.CompilerParams(vmem_limit_bytes=24 * 1024 * 1024),
        cost_estimate=pl.CostEstimate(flops=8 * TOK * width * 2 * COLS, bytes_accessed=3_500_000, transcendentals=0),
    )(*args)


def body(w_local, anchor, momentum, key_grad):
    r = lax.axis_index("replica")
    f = lax.axis_index("fsdp")
    t = lax.axis_index("tensor")
    ix = jnp.stack([r & 3, r >> 4, (r >> 2) & 3, f, t])
    w = w_local[0]
    mom = momentum[0, 0]
    top = (TOP, F32)

    def bf(n):
        return ((n, COLS), BF16)

    def fl(n):
        return ((n, COLS), F32)

    w_other = swap(w, "tensor", 1)
    four = (8, 4, ROWS, COLS)
    m1, m2, m3, own, a_y, kgm, mx = call(
        start_kernel,
        [bf(320)] * 3 + [fl(320)] * 2 + [bf(304), top],
        (ix, w.reshape(four), anchor.reshape(four), key_grad[0]),
    )
    kg_far = swap(kgm, "fsdp", 4)
    g2, g1, g3 = (swap(m, "replica", d) for d, m in ((2, m2), (1, m1), (3, m3)))
    h, own4 = call(y_kernel, [bf(160), fl(160)], (ix, own, a_y, g1, g2, g3), [fl(320)])
    theirs, kg_mine, mx = call(pair_kernel, [bf(304), bf(288), top], (ix, kgm, kg_far, mx))
    h = swap(h, "replica", 4)
    kg_core = swap(theirs, "tensor", 1)
    h, own2 = call(near_kernel, [bf(80), fl(80)], (ix, own4, h))
    h = swap(h, "replica", 8)
    both, ms = call(core_kernel, [bf(576), ((8, 128), F32)], (ix, kg_mine, kg_core, mx))
    ms = jnp.maximum(ms, swap(ms, "fsdp", 1))
    mr = swap(ms, "fsdp", 3)
    kg_x = swap(tie(both, (h, ms)), "fsdp", 1)
    wide = [jnp.concatenate([m, m], axis=1) for m in (ms, mr)]
    q, p_own, mx = call(lo_kernel, [bf(96), fl(40), top], (ix, own2, mom, h, *wide), [fl(80)])
    g = swap(q, "replica", 16)
    fresh, mom_new, mx = call(hi_kernel, [bf(96), fl(40), top], (ix, q, p_own, mom, a_y, mx, g), [fl(80)], 14.0)
    f3, f2, f1 = (swap(fresh, "replica", 4 * d) for d in (3, 2, 1))
    quad = call(quad_kernel, [bf(1152)], (ix, both, tie(kg_x, q)))[0]
    more = swap(quad, "fsdp", 3)
    place = jnp.array([0, 4, 1, 5, 3, 7, 2, 6], jnp.int32) ^ f
    prod = product(place[:4], quad, w, w_other)
    eight, mx = call(eight_kernel, [bf(336), top], (ix, fresh, f1, f2, tie(f3, prod), mx), [fl(320)])
    e2, e1, e3 = (swap(eight, "replica", d) for d in (2, 1, 3))
    prod = product(place[4:], tie(more, eight), w, w_other, prod)
    new_weights, scale = call(out_kernel, [(four, BF16), ((1, 1), F32)], (ix, eight, e1, e2, tie(e3, prod), mx))
    return new_weights.reshape(anchor.shape), mom_new[None, None], prod[None], scale.reshape(1)


def solution(mesh):
    return jax.shard_map(
        body,
        mesh=mesh,
        in_specs=(
            P("replica", "fsdp", "tensor"),
            P("fsdp", "tensor"),
            P("fsdp", "replica", None, "tensor"),
            P("replica", "fsdp", "tensor"),
        ),
        out_specs=(
            P("fsdp", "tensor"),
            P("fsdp", "replica", None, "tensor"),
            P("replica", None, "tensor", "fsdp"),
            P(),
        ),
        check_vma=False,
    )
```
